512 devices in a mesh: ctx: 128 (over z, y, core), tp: 4 (over x).
Axes of the slice: x: 4, y: 4, z: 16, core: 2. Of those that a mesh axis runs over, the one named last changes fastest.
Arguments:
- query: bfloat16 [32768, 4096], P('ctx', 'tp'), may hold values from -6 to 6
- key: bfloat16 [32768, 4096], P('ctx', 'tp'), may hold values from -6 to 6
- value: bfloat16 [32768, 4096], P('ctx', 'tp'), may hold values from -68 to 68
- gain: float32 [4096], P('tp'), may hold values from 0.1 to 1.9
- grad_out: bfloat16 [32768, 4096], P('ctx', 'tp'), may hold values from -6 to 6
Outputs:
- grad_query: bfloat16 [32768, 4096], P('ctx', 'tp')
- grad_key: bfloat16 [32768, 4096], P('ctx', 'tp')
- grad_value: bfloat16 [32768, 4096], P('ctx', 'tp')
The draws below stay inside these ranges and needn't reach their ends.
All inputs are finite; a program needn't handle non-finite values.
Results may differ from the reference program's by a relative error of at most 0.0065.
Values sent between devices are 32-bit elements; how exact they have to be, the bound alone decides.
A program may use at most 64 MiB of HBM per device.

```python
import jax
import jax.numpy as jnp
from jax import lax

HEAD = 128
HEADS = 32
BLOCK = 256
TOKENS = 32768
WIN = 4096


def draw_value(key, part):
    key = jax.random.fold_in(key, 7)
    factor_key, entry_key = jax.random.split(key)
    factor = jax.random.uniform(factor_key, (HEADS,), jnp.float32, 0.8, 1.25)
    which = jnp.arange(WIN) // HEAD
    frac = which.astype(jnp.float32) / (HEADS - 1)
    scale = 0.3 * jnp.power(10.0, frac) * factor[which]
    entries = jnp.clip(jax.random.normal(entry_key, (TOKENS, WIN), jnp.float32), -6.0, 6.0)
    return (entries * scale[None, :]).astype(jnp.bfloat16)


def shard_levels(stream_key, shape, cuts, low, top_value):
    loudness, own = 1.0, jax.random.fold_in(stream_key, 6)
    for position, shards_of in cuts:
        heights = jnp.exp(jax.random.uniform(jax.random.fold_in(own, position), (shards_of,), jnp.float32, low / len(cuts), top_value / len(cuts)))
        loudness = loudness * jnp.repeat(heights, shape[position] // shards_of).reshape([-1 if axis == position else 1 for axis in range(len(shape))])
    return loudness


def noise(stream_key, dims, width, limit, shards=(), dtype=jnp.bfloat16):
    loudness = shard_levels(stream_key, dims, shards, -0.22, 0.18) if shards else 1.0
    array = jax.random.normal(stream_key, dims, jnp.float32) * width * loudness
    return jnp.minimum(jnp.maximum(array, -limit), limit).astype(dtype)


def setup_inputs(seed: int = 0) -> dict:
    splits = jax.random.split(jax.random.key(seed), 6)
    return {
        "query": noise(splits[0], (TOKENS, WIN), 1.0, 6.0, ((0, 128), (1, 4))),
        "key": noise(splits[1], (TOKENS, WIN), 1.0, 6.0, ((0, 128), (1, 4))),
        "value": draw_value(jax.random.fold_in(splits[5], 71), 0),
        "gain": jnp.clip(1.0 + 0.18 * jax.random.normal(splits[3], (WIN,), jnp.float32), 0.1, 1.9),
        "grad_out": noise(splits[4], (TOKENS, WIN), 1.0, 6.0, ((0, 128), (1, 4))),
    }


def unit_rows(raw):
    wide = raw.astype(jnp.float32).reshape(TOKENS, HEADS, HEAD)
    length = jnp.sqrt(lax.optimization_barrier(jnp.sum(wide * wide, -1, keepdims=True)) + 1e-06)
    return (wide / length, length)

def rounded(values):
    return lax.optimization_barrier(values.astype(jnp.bfloat16)).astype(jnp.float32)

def reference(query, key, value, gain, grad_out):
    top = lax.Precision.HIGHEST
    count = TOKENS // BLOCK
    q_unit, q_norm = unit_rows(query)
    k_unit, k_norm = unit_rows(key)
    q_b = rounded(q_unit).reshape(count, BLOCK, HEADS, HEAD)
    k_b = rounded(k_unit).reshape(count, BLOCK, HEADS, HEAD)
    v_wide = value.astype(jnp.float32).reshape(count, BLOCK, HEADS, HEAD)
    lower = jnp.tril(jnp.ones((BLOCK, BLOCK), jnp.float32))
    empty = jnp.zeros((HEADS, HEAD, HEAD), jnp.float32)

    def forward(state, pieces):
        q_blk, k_blk, v_blk = pieces
        scores = jnp.einsum('thd,shd->hts', q_blk, k_blk, precision=top) * lower
        scores_b = rounded(scores)
        out = jnp.einsum('hts,she->the', scores_b, v_blk, precision=top)
        out = out + jnp.einsum('thd,hde->the', q_blk, state, precision=top)
        grown = state + jnp.einsum('shd,she->hde', k_blk, v_blk, precision=top)
        return (grown, (out, state))
    _, (attended, prior) = lax.scan(forward, empty, (q_b, k_b, v_wide))
    flat = attended.reshape(TOKENS, WIN)
    rms = jnp.sqrt(lax.optimization_barrier(jnp.mean(flat * flat, -1)) + 1e-05)
    weighted = grad_out.astype(jnp.float32) * gain
    cross = lax.optimization_barrier(jnp.sum(weighted * flat, -1))
    d_att = weighted / rms[:, None] - flat * (cross / (WIN * rms * rms * rms))[:, None]
    d_b = rounded(d_att).reshape(count, BLOCK, HEADS, HEAD)

    def backward(state, pieces):
        q_blk, k_blk, v_blk, d_blk, p_blk = pieces
        scores_b = rounded(jnp.einsum('thd,shd->hts', q_blk, k_blk, precision=top) * lower)
        d_scores_b = rounded(jnp.einsum('the,she->hts', d_blk, v_blk, precision=top) * lower)
        d_q = jnp.einsum('hts,shd->thd', d_scores_b, k_blk, precision=top)
        d_q = d_q + jnp.einsum('the,hde->thd', d_blk, p_blk, precision=top)
        d_k = jnp.einsum('hts,thd->shd', d_scores_b, q_blk, precision=top)
        d_k = d_k + jnp.einsum('she,hde->shd', v_blk, state, precision=top)
        d_v = jnp.einsum('hts,the->she', scores_b, d_blk, precision=top)
        d_v = d_v + jnp.einsum('shd,hde->she', k_blk, state, precision=top)
        grown = state + jnp.einsum('thd,the->hde', q_blk, d_blk, precision=top)
        return (grown, (d_q, d_k, d_v))
    _, (d_q, d_k, d_v) = lax.scan(backward, empty, (q_b, k_b, v_wide, d_b, prior), reverse=True)
    d_q = d_q.reshape(TOKENS, HEADS, HEAD)
    d_k = d_k.reshape(TOKENS, HEADS, HEAD)
    grad_query = (d_q - q_unit * lax.optimization_barrier(jnp.sum(q_unit * d_q, -1, keepdims=True))) / q_norm
    grad_key = (d_k - k_unit * lax.optimization_barrier(jnp.sum(k_unit * d_k, -1, keepdims=True))) / k_norm
    return (grad_query.reshape(TOKENS, WIN).astype(jnp.bfloat16), grad_key.reshape(TOKENS, WIN).astype(jnp.bfloat16), d_v.reshape(TOKENS, WIN).astype(jnp.bfloat16))
```

```python
import jax
import jax.numpy as jnp
from jax import lax
from jax.experimental import pallas as pl
from jax.experimental.pallas import tpu as pltpu
from jax.sharding import PartitionSpec as P

HEAD = 128
BLOCK = 256
HEADS = 8
HALF = 4
NY = 4
NZ = 16
NX = 4
ROWS = HEAD // NZ
F32 = jnp.float32
BF16 = jnp.bfloat16
MESH = pl.DeviceIdType.MESH
FAR_FIRST = sorted(range(1, NZ), key=lambda d: -min(d, NZ - d))

NN = (((1,), (0,)), ((), ()))
NT = (((1,), (1,)), ((), ()))
TN = (((0,), (0,)), ((), ()))


def dot(a, b, dims):
    return lax.dot_general(a, b, dims, preferred_element_type=F32)


def split(wide, axis):
    high = wide.astype(BF16)
    low = (wide - high.astype(F32)).astype(BF16)
    return jnp.concatenate([high, low], axis)


def twice(narrow):
    return jnp.concatenate([narrow, narrow], 1)


class Place:
    def __init__(self):
        ctx = lax.axis_index("ctx")
        self.x = lax.axis_index("tp")
        self.z = lax.div(ctx, 2 * NY)
        self.y = lax.rem(lax.div(ctx, 2), NY)
        self.core = lax.rem(ctx, 2)

    def at(self, z=None, y=None, core=None, x=None):
        z = self.z if z is None else z
        y = self.y if y is None else y
        core = self.core if core is None else core
        x = self.x if x is None else x
        return ((z * NY + y) * 2 + core, x)


def remote(src, dst, send, recv, device):
    return pltpu.make_async_remote_copy(
        src_ref=src, dst_ref=dst, send_sem=send, recv_sem=recv, device_id=device, device_id_type=MESH
    )


class Scan:
    def __init__(self, me, state, bufs, reverse):
        (self.other, self.chip, self.plane, self.ahead, self.total, self.planes, self.sums, self.base,
         self.out, self.mine, self.fore, self.result, self.sems) = bufs
        self.me, self.state, self.reverse = me, state, reverse
        self.sends = []

    def sem(self, slot):
        return self.sems.at[0, slot], self.sems.at[1, slot]

    def order(self, count):
        return reversed(range(count)) if self.reverse else range(count)

    def go(self, copy):
        copy.start()
        self.sends.append(copy)
        return copy

    def head_copy(self, d):
        me = self.me
        s = lax.rem(me.y + d, NY)
        return remote(
            self.state.at[HALF * (1 - me.core) + s], self.other.at[s], *self.sem(d), me.at(core=1 - me.core)
        )

    def send_head(self, d):
        self.go(self.head_copy(d))

    def y_phase(self):
        me = self.me
        waits = []
        for d in (1, 2, 3, 0):
            s = lax.rem(me.y + d, NY)
            self.head_copy(d).wait_recv()
            whole = self.state[HALF * me.core + s] + self.other[s]
            if d:
                self.chip[s] = whole
                waits.append(self.go(remote(
                    self.chip.at[s], self.plane.at[me.y], *self.sem(4 + d), me.at(y=s)
                )))
            else:
                self.plane[s] = whole
        for copy in waits:
            copy.wait_recv()
        run = jnp.zeros((HEAD, HEAD), F32)
        for y in self.order(NY):
            self.ahead[y] = run
            run = run + self.plane[y]
        self.total[...] = run.reshape(NZ, ROWS, HEAD)

    def z_send(self):
        me = self.me
        self.z_waits = []
        for d in FAR_FIRST:
            z = lax.rem(me.z + d, NZ)
            self.z_waits.append(self.go(remote(
                self.total.at[z], self.planes.at[me.z], *self.sem(8 + d), me.at(z=z)
            )))
        self.planes[me.z] = self.total[me.z]

    def z_back(self):
        me = self.me
        for copy in self.z_waits:
            copy.wait_recv()
        run = jnp.zeros((ROWS, HEAD), F32)
        for z in self.order(NZ):
            self.sums[z] = run
            run = run + self.planes[z]
        waits = []
        for d in FAR_FIRST:
            z = lax.rem(me.z + d, NZ)
            waits.append(self.go(remote(
                self.sums.at[z], self.base.at[me.z], *self.sem(24 + d), me.at(z=z)
            )))
        self.base[me.z] = self.sums[me.z]
        for copy in waits:
            copy.wait_recv()

    def y_back(self):
        me = self.me
        base = self.base[...].reshape(HEAD, HEAD)
        waits = []
        for d in (2, 1, 3):
            y = lax.rem(me.y + d, NY)
            self.out[y] = self.ahead[y] + base
            waits.append((d, self.go(remote(
                self.out.at[y], self.mine.at[me.y], *self.sem(40 + d), me.at(y=y)
            ))))
        self.mine[me.y] = self.ahead[me.y] + base
        first = 1 if self.reverse else 0
        for d, copy in [(0, None)] + waits:
            s = lax.rem(me.y - d + NY, NY)
            if copy is not None:
                copy.wait_recv()
            head = HALF * me.core + s
            got = self.mine[s]
            leads = me.core == first
            self.fore[s] = got + jnp.where(leads, self.state[head], 0.0)
            self.result[head] = got + jnp.where(leads, 0.0, self.other[s])
            self.go(remote(
                self.fore.at[s], self.result.at[head], *self.sem(44 + d), me.at(core=1 - me.core)
            ))

    def result_slot(self, i):
        me = self.me
        d = (0, 2, 1, 3)[i % HALF]
        s = lax.rem(me.y - d + NY, NY)
        if i < HALF:
            return HALF * me.core + s
        head = HALF * (1 - me.core) + s
        remote(
            self.fore.at[s], self.result.at[head], *self.sem(44 + d), me.at(core=1 - me.core)
        ).wait_recv()
        return head

    def finish(self):
        for copy in self.sends:
            copy.wait_send()


def columns(head):
    if isinstance(head, int):
        return pl.ds(head * HEAD, HEAD)
    return pl.ds(pl.multiple_of(head * HEAD, HEAD), HEAD)


def kernel(
    q_hbm, k_hbm, v_hbm, gain_ref, g_hbm, dq_hbm, dk_hbm, dv_hbm,
    q_raw, k_raw, v_b, g_raw, q_b, k_b, q_inv, k_inv, att, wei, d_b, scores_b, dk_part, dv_part,
    prior_s, own_s, sums_s, dq_o, dk_o, dv_o, load_sems, store_sems, x_sems, *scan_bufs,
):
    me = Place()
    loads = [
        pltpu.make_async_copy(src, dst, load_sems.at[i])
        for i, (src, dst) in enumerate(((k_hbm, k_raw), (v_hbm, v_b), (q_hbm, q_raw), (g_hbm, g_raw)))
    ]
    for copy in loads:
        copy.start()
    barrier = pltpu.get_barrier_semaphore()
    peers = [me.at(core=1 - me.core)]
    peers += [me.at(z=lax.rem(me.z + d, NZ)) for d in FAR_FIRST]
    peers += [me.at(y=lax.rem(me.y + d, NY)) for d in (2, 1, 3)]
    peers += [me.at(x=lax.rem(me.x + d, NX)) for d in (2, 1, 3)]
    for peer in peers:
        pl.semaphore_signal(barrier, inc=1, device_id=peer, device_id_type=MESH)

    count = len(scan_bufs) // 2
    fore = Scan(me, own_s.at[0], scan_bufs[:count], False)
    back = Scan(me, own_s.at[1], scan_bufs[count:], True)

    def send_order(i):
        s = lax.rem(me.y + (1, 2, 3, 0)[i % HALF], NY)
        return s + HALF * ((1 - me.core) if i < HALF else me.core)

    loads[0].wait()
    loads[1].wait()
    for i in range(HEADS):
        head = send_order(i)
        cols = columns(head)
        wide = k_raw[:, cols].astype(F32)
        inv = lax.rsqrt(jnp.sum(wide * wide, -1, keepdims=True) + 1e-06)
        k_inv[head] = jnp.broadcast_to(inv, (BLOCK, HEAD))
        unit = (wide * inv).astype(BF16)
        k_b[:, cols] = unit
        own_s[0, head] = dot(unit, v_b[:, cols], TN)
    pl.semaphore_wait(barrier, len(peers))
    for d in (1, 2, 3, 0):
        fore.send_head(d)
    fore.y_phase()
    fore.z_send()

    loads[2].wait()
    loads[3].wait()
    lower = lax.broadcasted_iota(jnp.int32, (BLOCK, BLOCK), 0) >= lax.broadcasted_iota(jnp.int32, (BLOCK, BLOCK), 1)
    for head in range(HEADS):
        cols = columns(head)
        wide = q_raw[:, cols].astype(F32)
        inv = lax.rsqrt(jnp.sum(wide * wide, -1, keepdims=True) + 1e-06)
        q_inv[head] = jnp.broadcast_to(inv, (BLOCK, HEAD))
        unit = (wide * inv).astype(BF16)
        q_b[:, cols] = unit
        scores = jnp.where(lower, dot(unit, k_b[:, cols], NT), 0.0).astype(BF16)
        scores_b[head] = scores
        att[head] = dot(scores, v_b[:, cols], NN)
        wei[head] = g_raw[:, cols].astype(F32) * gain_ref[:, cols]
    fore.z_back()
    fore.y_back()

    square = jnp.zeros((BLOCK, HEAD), F32)
    cross = jnp.zeros((BLOCK, HEAD), F32)
    for i in range(HEADS):
        head = fore.result_slot(i)
        both = split(fore.result[head], 0)
        prior_s[head] = both
        out = att[head] + dot(twice(q_b[:, columns(head)]), both, NN)
        att[head] = out
        square = square + out * out
        cross = cross + wei[head] * out
    lane = lax.broadcasted_iota(jnp.int32, (BLOCK, HEAD), 1)
    pair = jnp.where(
        lane == 0, jnp.sum(square, -1, keepdims=True), jnp.sum(cross, -1, keepdims=True)
    )
    sums_s[0] = pair.T[:8]
    x_waits = []
    for d in (2, 1, 3):
        copy = remote(
            sums_s.at[0], sums_s.at[d], x_sems.at[0, d], x_sems.at[1, d], me.at(x=lax.rem(me.x + d, NX))
        )
        copy.start()
        x_waits.append(copy)
    for copy in x_waits:
        copy.wait_recv()
    total = (sums_s[0] + sums_s[1]) + (sums_s[2] + sums_s[3])
    full = NX * HEADS * HEAD
    scale = lax.rsqrt(total[0:1] / full + 1e-05)
    slope = total[1:2] * (scale * scale * scale) / full
    row = lax.broadcasted_iota(jnp.int32, (HEAD, BLOCK), 0)
    factors = jnp.where(row == 0, scale, slope).T
    scale, slope = factors[:, 0:1], factors[:, 1:2]

    for i in range(HEADS):
        head = send_order(i)
        cols = columns(head)
        grad = (wei[head] * scale - att[head] * slope).astype(BF16)
        d_b[:, cols] = grad
        own_s[1, head] = dot(q_b[:, cols], grad, TN)
        if i < HALF:
            back.send_head((1, 2, 3, 0)[i])
    back.y_phase()
    back.z_send()

    for head in range(HEADS):
        cols = columns(head)
        grad = d_b[:, cols]
        keys = k_b[:, cols]
        d_scores = jnp.where(lower, dot(grad, v_b[:, cols], NT), 0.0).astype(BF16)
        d_q = dot(d_scores, keys, NN)
        both = prior_s[head]
        d_q = d_q + dot(twice(grad), jnp.concatenate([both[:HEAD], both[HEAD:]], 1), NT)
        inv = q_inv[head]
        unit = q_raw[:, cols].astype(F32) * inv
        d_q = (d_q - unit * jnp.sum(unit * d_q, -1, keepdims=True)) * inv
        dq_o[:, cols] = d_q.astype(BF16)
        dk_part[head] = dot(d_scores, q_b[:, cols], TN)
        dv_part[head] = dot(scores_b[head], grad, TN)
    stores = [pltpu.make_async_copy(dq_o, dq_hbm, store_sems.at[0])]
    stores[0].start()
    back.z_back()
    back.y_back()

    for i in range(HEADS):
        head = back.result_slot(i)
        cols = columns(head)
        state = back.result[head]
        keys = k_b[:, cols]
        d_v = dv_part[head] + dot(twice(keys), split(state, 0), NN)
        dv_o[:, cols] = d_v.astype(BF16)
        d_k = dk_part[head] + dot(twice(v_b[:, cols]), split(state, 1), NT)
        inv = k_inv[head]
        unit = k_raw[:, cols].astype(F32) * inv
        d_k = (d_k - unit * jnp.sum(unit * d_k, -1, keepdims=True)) * inv
        dk_o[:, cols] = d_k.astype(BF16)
    stores.append(pltpu.make_async_copy(dk_o, dk_hbm, store_sems.at[1]))
    stores.append(pltpu.make_async_copy(dv_o, dv_hbm, store_sems.at[2]))
    for copy in stores[1:]:
        copy.start()
    fore.finish()
    back.finish()
    for copy in x_waits:
        copy.wait_send()
    for copy in stores:
        copy.wait()


def scan_scratch():
    square = pltpu.VMEM((HALF, HEAD, HEAD), F32)
    pieces = pltpu.VMEM((NZ, ROWS, HEAD), F32)
    return [
        square, square, square, square, pieces, pieces, pieces, pieces, square, square, square,
        pltpu.VMEM((HEADS, HEAD, HEAD), F32), pltpu.SemaphoreType.DMA((2, 48)),
    ]


def body(query, key, value, gain, grad_out):
    rows, width = query.shape
    flat = pltpu.VMEM((rows, width), BF16)
    wide = pltpu.VMEM((HEADS, rows, HEAD), F32)
    out = jax.ShapeDtypeStruct((rows, width), BF16)
    hbm = pl.BlockSpec(memory_space=pl.ANY)
    vmem = pl.BlockSpec(memory_space=pltpu.VMEM)
    return pl.pallas_call(
        kernel,
        out_shape=(out, out, out),
        in_specs=[hbm, hbm, hbm, vmem, hbm],
        out_specs=(hbm, hbm, hbm),
        scratch_shapes=[
            flat, flat, flat, flat, flat, flat, wide, wide, wide, wide, flat,
            pltpu.VMEM((HEADS, rows, rows), BF16), wide, wide,
            pltpu.VMEM((HEADS, 2 * HEAD, HEAD), BF16),
            pltpu.VMEM((2, HEADS, HEAD, HEAD), F32),
            pltpu.VMEM((NX, 8, rows), F32),
            flat, flat, flat,
            pltpu.SemaphoreType.DMA((4,)), pltpu.SemaphoreType.DMA((3,)), pltpu.SemaphoreType.DMA((2, NX)),
        ] + scan_scratch() + scan_scratch(),
        compiler_params=pltpu.CompilerParams(
            collective_id=0, has_side_effects=True, vmem_limit_bytes=40 << 20
        ),
        name="linear_attention_backward",
    )(query, key, value, gain.reshape(1, width), grad_out)


def solution(mesh):
    placed = (P("ctx", "tp"), P("ctx", "tp"), P("ctx", "tp"), P("tp"), P("ctx", "tp"))
    return jax.shard_map(
        body,
        mesh=mesh,
        in_specs=placed,
        out_specs=(P("ctx", "tp"), P("ctx", "tp"), P("ctx", "tp")),
        check_vma=False,
    )
```

```python
import jax
import jax.numpy as jnp
from jax import lax
from jax.experimental import pallas as pl
from jax.experimental.pallas import tpu as pltpu
from jax.sharding import PartitionSpec as P

HEAD = 128
BLOCK = 256
HEADS = 8
HALF = 4
NY = 4
NZ = 16
NX = 4
SLICES = 8
DEPTH = HEAD // SLICES
CHUNKS = 2
PART = SLICES // CHUNKS
F32 = jnp.float32
BF16 = jnp.bfloat16
MESH = pl.DeviceIdType.MESH
FAR_FIRST = sorted(range(1, NZ), key=lambda d: -min(d, NZ - d))
BACK_SLOT = {e: (2 - e) % SLICES for e in range(-4, 4)}
SHARE_ORDER = (0, 1, 3, 2)
SEND_ORDER = (2, 1, 3, 0)

NN = (((1,), (0,)), ((), ()))
NT = (((1,), (1,)), ((), ()))
TN = (((0,), (0,)), ((), ()))


def dot(a, b, dims):
    return lax.dot_general(a, b, dims, preferred_element_type=F32)


def split(wide, axis):
    high = wide.astype(BF16)
    low = (wide - high.astype(F32)).astype(BF16)
    return jnp.concatenate([high, low], axis)


def twice(narrow):
    return jnp.concatenate([narrow, narrow], 1)


class Place:
    def __init__(self):
        ctx = lax.axis_index("ctx")
        self.x = lax.axis_index("tp")
        self.z = lax.div(ctx, 2 * NY)
        self.y = lax.rem(lax.div(ctx, 2), NY)
        self.core = lax.rem(ctx, 2)

    def at(self, z=None, y=None, core=None, x=None):
        z = self.z if z is None else z
        y = self.y if y is None else y
        core = self.core if core is None else core
        x = self.x if x is None else x
        return ((z * NY + y) * 2 + core, x)


def remote(src, dst, send, recv, device):
    return pltpu.make_async_remote_copy(
        src_ref=src, dst_ref=dst, send_sem=send, recv_sem=recv, device_id=device, device_id_type=MESH
    )


def hops(d):
    return min(d % NZ, -d % NZ)


def shift(slot):
    return (slot + 6) % SLICES


class Scan:
    def __init__(self, me, state, bufs, reverse):
        (self.other, self.chip, self.plane, self.ahead, self.total, self.planes, self.sums, self.base,
         self.out, self.mine, self.fore, self.result, self.core_sems, self.y_sems, self.z_sems, self.zb_sems,
         self.yb_sems, self.share_sems) = bufs
        self.me, self.state, self.reverse = me, state, reverse
        self.sends = []

    def order(self, count):
        return reversed(range(count)) if self.reverse else range(count)

    def go(self, copy):
        copy.start()
        self.sends.append(copy)
        return copy

    def slice_at(self, slot):
        return lax.rem(self.me.z + shift(slot), SLICES)

    def slot_of(self, j):
        return lax.rem(2 * SLICES + j - 6 - lax.rem(self.me.z, SLICES), SLICES)

    def head_copy(self, d):
        me = self.me
        s = lax.rem(me.y + d, NY)
        return remote(
            self.state.at[HALF * (1 - me.core) + s], self.other.at[s], self.core_sems.at[0, d],
            self.core_sems.at[1, d], me.at(core=1 - me.core)
        )

    def send_head(self, d):
        self.go(self.head_copy(d))

    def y_copy(self, chunk, d):
        me = self.me
        s = lax.rem(me.y + d, NY)
        part = pl.ds(chunk * PART, PART)
        return remote(
            self.chip.at[s, part], self.plane.at[me.y, part], self.y_sems.at[0, chunk, d],
            self.y_sems.at[1, chunk, d], me.at(y=s)
        )

    def y_send(self):
        me = self.me
        for chunk in range(CHUNKS):
            for d in (2, 1, 3, 0):
                s = lax.rem(me.y + d, NY)
                if chunk == 0:
                    self.head_copy(d).wait_recv()
                for slot in range(chunk * PART, chunk * PART + PART):
                    j = self.slice_at(slot)
                    whole = self.state[HALF * me.core + s, j] + self.other[s, j]
                    if d:
                        self.chip[s, slot] = whole
                    else:
                        self.plane[me.y, slot] = whole
                if d:
                    self.go(self.y_copy(chunk, d))

    def z_copy(self, slot, d):
        me = self.me
        d = d % NZ
        z = lax.rem(me.z + d, NZ)
        return remote(
            self.total.at[slot], self.planes.at[me.z], self.z_sems.at[0, d], self.z_sems.at[1, d], me.at(z=z)
        )

    def z_send(self):
        me = self.me
        for chunk in range(CHUNKS):
            for d in (1, 3, 2):
                self.y_copy(chunk, d).wait_recv()
            slots = range(chunk * PART, chunk * PART + PART)
            for slot in slots:
                run = jnp.zeros((DEPTH, HEAD), F32)
                for y in self.order(NY):
                    self.ahead[y, slot] = run
                    run = run + self.plane[y, slot]
                self.total[slot] = run
            targets = [(slot, shift(slot) + far) for slot in slots for far in (0, SLICES)]
            for slot, d in sorted(targets, key=lambda t: -hops(t[1])):
                if d:
                    self.go(self.z_copy(slot, d))
                else:
                    self.planes[me.z] = self.total[slot]

    def zb_copy(self, e):
        me = self.me
        z = lax.rem(me.z + e + NZ, NZ)
        return remote(
            self.sums.at[z], self.base.at[BACK_SLOT[e]], self.zb_sems.at[0, BACK_SLOT[e]],
            self.zb_sems.at[1, BACK_SLOT[e]], me.at(z=z)
        )

    def z_back(self):
        me = self.me
        for d in sorted(range(1, NZ), key=hops):
            self.z_copy(0, d).wait_recv()
        run = jnp.zeros((DEPTH, HEAD), F32)
        for z in self.order(NZ):
            self.sums[z] = run
            run = run + self.planes[z]
        for e in sorted(BACK_SLOT, key=lambda e: -abs(e)):
            if e:
                self.go(self.zb_copy(e))
        self.base[BACK_SLOT[0]] = self.sums[me.z]

    def yb_copy(self, chunk, d):
        me = self.me
        y = lax.rem(me.y + d, NY)
        part = pl.ds(chunk * PART, PART)
        return remote(
            self.out.at[y, part], self.mine.at[me.y, part], self.yb_sems.at[0, chunk, d],
            self.yb_sems.at[1, chunk, d], me.at(y=y)
        )

    def share_copy(self, chunk, d):
        me = self.me
        s = lax.rem(me.y - d + NY, NY)
        part = pl.ds(chunk * PART, PART)
        return remote(
            self.fore.at[s, part], self.result.at[HALF * me.core + s, part], self.share_sems.at[0, chunk, d],
            self.share_sems.at[1, chunk, d], me.at(core=1 - me.core)
        )

    def y_back(self):
        me = self.me
        leads = me.core == (1 if self.reverse else 0)
        for chunk in range(CHUNKS):
            slots = range(chunk * PART, chunk * PART + PART)
            for e, slot in sorted(BACK_SLOT.items(), key=lambda t: abs(t[0])):
                if e and slot in slots:
                    self.zb_copy(e).wait_recv()
            for d in (2, 1, 3, 0):
                y = lax.rem(me.y + d, NY)
                for slot in slots:
                    value = self.ahead[y, slot] + self.base[slot]
                    if d:
                        self.out[y, slot] = value
                    else:
                        self.mine[y, slot] = value
                if d:
                    self.go(self.yb_copy(chunk, d))
        for chunk in range(CHUNKS):
            slots = range(chunk * PART, chunk * PART + PART)
            for d in SHARE_ORDER:
                if d:
                    self.yb_copy(chunk, d).wait_recv()
                s = lax.rem(me.y - d + NY, NY)
                head = HALF * me.core + s
                for slot in slots:
                    j = self.slice_at(slot)
                    got = self.mine[s, slot]
                    self.fore[s, slot] = got + jnp.where(leads, self.state[head, j], 0.0)
                    self.result[head, slot] = got + jnp.where(leads, 0.0, self.other[s, j])
                self.go(self.share_copy(chunk, d))

    def result_head(self, i):
        me = self.me
        d = SHARE_ORDER[i % HALF]
        s = lax.rem(me.y - d + NY, NY)
        if i < HALF:
            return HALF * me.core + s
        for chunk in range(CHUNKS):
            self.share_copy(chunk, d).wait_recv()
        return HALF * (1 - me.core) + s

    def result_state(self, head):
        return jnp.concatenate([self.result[head, self.slot_of(j)] for j in range(SLICES)], 0)

    def finish(self):
        for copy in self.sends:
            copy.wait_send()


def columns(head):
    if isinstance(head, int):
        return pl.ds(head * HEAD, HEAD)
    return pl.ds(pl.multiple_of(head * HEAD, HEAD), HEAD)


def kernel(
    q_hbm, k_hbm, v_hbm, gain_hbm, g_hbm, dq_hbm, dk_hbm, dv_hbm,
    q_raw, k_raw, v_b, g_raw, gain_ref, q_b, k_b, q_inv, k_inv, att, wei, d_b, scores_b, dk_part, dv_part,
    prior_s, own_s, sums_s, dq_o, dk_o, dv_o, load_sems, store_sems, x_sems, *scan_bufs,
):
    me = Place()
    loads = [
        pltpu.make_async_copy(src, dst, load_sems.at[i])
        for i, (src, dst) in enumerate(((k_hbm, k_raw), (v_hbm, v_b), (q_hbm, q_raw), (g_hbm, g_raw), (gain_hbm, gain_ref)))
    ]
    for copy in loads:
        copy.start()
    barrier = pltpu.get_barrier_semaphore()
    peers = [me.at(core=1 - me.core)]
    peers += [me.at(z=lax.rem(me.z + d, NZ)) for d in FAR_FIRST]
    peers += [me.at(y=lax.rem(me.y + d, NY)) for d in (2, 1, 3)]
    peers += [me.at(x=lax.rem(me.x + d, NX)) for d in (2, 1, 3)]
    for peer in peers:
        pl.semaphore_signal(barrier, inc=1, device_id=peer, device_id_type=MESH)

    count = len(scan_bufs) // 2
    fore = Scan(me, own_s.at[0], scan_bufs[:count], False)
    back = Scan(me, own_s.at[1], scan_bufs[count:], True)

    def send_order(i):
        s = lax.rem(me.y + SEND_ORDER[i % HALF], NY)
        return s + HALF * ((1 - me.core) if i < HALF else me.core)

    loads[0].wait()
    loads[1].wait()
    for i in range(HEADS):
        head = send_order(i)
        cols = columns(head)
        wide = k_raw[:, cols].astype(F32)
        inv = lax.rsqrt(jnp.sum(wide * wide, -1, keepdims=True) + 1e-06)
        k_inv[head] = jnp.broadcast_to(inv, (BLOCK, HEAD))
        unit = (wide * inv).astype(BF16)
        k_b[:, cols] = unit
        own_s[0, head] = dot(unit, v_b[:, cols], TN).reshape(SLICES, DEPTH, HEAD)
    pl.semaphore_wait(barrier, len(peers))
    for d in SEND_ORDER:
        fore.send_head(d)
    fore.y_send()
    fore.z_send()

    loads[2].wait()
    loads[3].wait()
    loads[4].wait()
    lower = lax.broadcasted_iota(jnp.int32, (BLOCK, BLOCK), 0) >= lax.broadcasted_iota(jnp.int32, (BLOCK, BLOCK), 1)
    for head in range(HEADS):
        cols = columns(head)
        wide = q_raw[:, cols].astype(F32)
        inv = lax.rsqrt(jnp.sum(wide * wide, -1, keepdims=True) + 1e-06)
        q_inv[head] = jnp.broadcast_to(inv, (BLOCK, HEAD))
        unit = (wide * inv).astype(BF16)
        q_b[:, cols] = unit
        scores = jnp.where(lower, dot(unit, k_b[:, cols], NT), 0.0).astype(BF16)
        scores_b[head] = scores
        att[head] = dot(scores, v_b[:, cols], NN)
        wei[head] = g_raw[:, cols].astype(F32) * gain_ref[:, cols]
    fore.z_back()
    fore.y_back()

    square = jnp.zeros((BLOCK, HEAD), F32)
    cross = jnp.zeros((BLOCK, HEAD), F32)
    for i in range(HEADS):
        head = fore.result_head(i)
        both = split(fore.result_state(head), 0)
        prior_s[head] = both
        out = att[head] + dot(twice(q_b[:, columns(head)]), both, NN)
        att[head] = out
        square = square + out * out
        cross = cross + wei[head] * out
    lane = lax.broadcasted_iota(jnp.int32, (BLOCK, HEAD), 1)
    pair = jnp.where(
        lane == 0, jnp.sum(square, -1, keepdims=True), jnp.sum(cross, -1, keepdims=True)
    )
    sums_s[0] = pair.T[:8]
    x_waits = []
    for d in (2, 1, 3):
        copy = remote(
            sums_s.at[0], sums_s.at[d], x_sems.at[0, d], x_sems.at[1, d], me.at(x=lax.rem(me.x + d, NX))
        )
        copy.start()
        x_waits.append(copy)
    for copy in x_waits:
        copy.wait_recv()
    total = (sums_s[0] + sums_s[1]) + (sums_s[2] + sums_s[3])
    full = NX * HEADS * HEAD
    scale = lax.rsqrt(total[0:1] / full + 1e-05)
    slope = total[1:2] * (scale * scale * scale) / full
    row = lax.broadcasted_iota(jnp.int32, (HEAD, BLOCK), 0)
    factors = jnp.where(row == 0, scale, slope).T
    scale, slope = factors[:, 0:1], factors[:, 1:2]

    for i in range(HEADS):
        head = send_order(i)
        cols = columns(head)
        grad = (wei[head] * scale - att[head] * slope).astype(BF16)
        d_b[:, cols] = grad
        own_s[1, head] = dot(q_b[:, cols], grad, TN).reshape(SLICES, DEPTH, HEAD)
        if i < HALF:
            back.send_head(SEND_ORDER[i])
    back.y_send()
    back.z_send()

    for head in range(HEADS):
        cols = columns(head)
        grad = d_b[:, cols]
        keys = k_b[:, cols]
        d_scores = jnp.where(lower, dot(grad, v_b[:, cols], NT), 0.0).astype(BF16)
        d_q = dot(d_scores, keys, NN)
        both = prior_s[head]
        d_q = d_q + dot(twice(grad), jnp.concatenate([both[:HEAD], both[HEAD:]], 1), NT)
        inv = q_inv[head]
        unit = q_raw[:, cols].astype(F32) * inv
        d_q = (d_q - unit * jnp.sum(unit * d_q, -1, keepdims=True)) * inv
        dq_o[:, cols] = d_q.astype(BF16)
        dk_part[head] = dot(d_scores, q_b[:, cols], TN)
        dv_part[head] = dot(scores_b[head], grad, TN)
    stores = [pltpu.make_async_copy(dq_o, dq_hbm, store_sems.at[0])]
    stores[0].start()
    back.z_back()
    back.y_back()

    for i in range(HEADS):
        head = back.result_head(i)
        cols = columns(head)
        state = back.result_state(head)
        keys = k_b[:, cols]
        d_v = dv_part[head] + dot(twice(keys), split(state, 0), NN)
        dv_o[:, cols] = d_v.astype(BF16)
        d_k = dk_part[head] + dot(twice(v_b[:, cols]), split(state, 1), NT)
        inv = k_inv[head]
        unit = k_raw[:, cols].astype(F32) * inv
        d_k = (d_k - unit * jnp.sum(unit * d_k, -1, keepdims=True)) * inv
        dk_o[:, cols] = d_k.astype(BF16)
    stores.append(pltpu.make_async_copy(dk_o, dk_hbm, store_sems.at[1]))
    stores.append(pltpu.make_async_copy(dv_o, dv_hbm, store_sems.at[2]))
    for copy in stores[1:]:
        copy.start()
    fore.finish()
    back.finish()
    for copy in x_waits:
        copy.wait_send()
    for copy in stores:
        copy.wait()


def scan_scratch():
    heads = pltpu.VMEM((HALF, SLICES, DEPTH, HEAD), F32)
    slices = pltpu.VMEM((SLICES, DEPTH, HEAD), F32)
    along_z = pltpu.VMEM((NZ, DEPTH, HEAD), F32)
    sems = pltpu.SemaphoreType.DMA
    return [
        heads, heads, heads, heads, slices, along_z, along_z, slices, heads, heads, heads,
        pltpu.VMEM((HEADS, SLICES, DEPTH, HEAD), F32),
        sems((2, NY)), sems((2, CHUNKS, NY)), sems((2, NZ)), sems((2, SLICES)), sems((2, CHUNKS, NY)),
        sems((2, CHUNKS, NY)),
    ]


def body(query, key, value, gain, grad_out):
    rows, width = query.shape
    flat = pltpu.VMEM((rows, width), BF16)
    wide = pltpu.VMEM((HEADS, rows, HEAD), F32)
    out = jax.ShapeDtypeStruct((rows, width), BF16)
    hbm = pl.BlockSpec(memory_space=pl.ANY)
    grads = pl.pallas_call(
        kernel,
        out_shape=(out, out, out),
        in_specs=[hbm] * 5,
        out_specs=(hbm, hbm, hbm),
        scratch_shapes=[
            flat, flat, flat, flat, pltpu.VMEM((1, width), F32), flat, flat, wide, wide, wide, wide, flat,
            pltpu.VMEM((HEADS, rows, rows), BF16), wide, wide,
            pltpu.VMEM((HEADS, 2 * HEAD, HEAD), BF16),
            pltpu.VMEM((2, HEADS, SLICES, DEPTH, HEAD), F32),
            pltpu.VMEM((NX, 8, rows), F32),
            flat, flat, flat,
            pltpu.SemaphoreType.DMA((5,)), pltpu.SemaphoreType.DMA((3,)), pltpu.SemaphoreType.DMA((2, NX)),
        ] + scan_scratch() + scan_scratch(),
        compiler_params=pltpu.CompilerParams(
            collective_id=0, has_side_effects=True, vmem_limit_bytes=52 << 20
        ),
        name="linear_attention_backward",
    )(query, key, value, gain.reshape(1, width), grad_out)
    return grads


def solution(mesh):
    placed = (P("ctx", "tp"), P("ctx", "tp"), P("ctx", "tp"), P("tp"), P("ctx", "tp"))
    return jax.shard_map(
        body,
        mesh=mesh,
        in_specs=placed,
        out_specs=(P("ctx", "tp"), P("ctx", "tp"), P("ctx", "tp")),
        check_vma=False,
    )
```

```python
import jax
import jax.numpy as jnp
from jax import lax
from jax.experimental import pallas as pl
from jax.experimental.pallas import tpu as pltpu
from jax.sharding import PartitionSpec as P

HEAD = 128
BLOCK = 256
HEADS = 8
HALF = 4
NY = 4
NZ = 16
NX = 4
SLICES = 8
REACH = 4
DEPTH = HEAD // SLICES
CHUNKS = 2
PART = SLICES // CHUNKS
F32 = jnp.float32
BF16 = jnp.bfloat16
MESH = pl.DeviceIdType.MESH
FAR_FIRST = sorted(range(1, NZ), key=lambda d: -min(d, NZ - d))
BACK_SLOT = {e: (2 - e) % SLICES for e in range(-4, 4)}
SHARE_ORDER = (0, 1, 3, 2)
SEND_ORDER = (2, 1, 3, 0)

NN = (((1,), (0,)), ((), ()))
NT = (((1,), (1,)), ((), ()))
TN = (((0,), (0,)), ((), ()))


def dot(a, b, dims):
    return lax.dot_general(a, b, dims, preferred_element_type=F32)


def split(wide, axis):
    high = wide.astype(BF16)
    low = (wide - high.astype(F32)).astype(BF16)
    return jnp.concatenate([high, low], axis)


def twice(narrow):
    return jnp.concatenate([narrow, narrow], 1)


class Place:
    def __init__(self):
        ctx = lax.axis_index("ctx")
        self.x = lax.axis_index("tp")
        self.z = lax.div(ctx, 2 * NY)
        self.y = lax.rem(lax.div(ctx, 2), NY)
        self.core = lax.rem(ctx, 2)

    def at(self, z=None, y=None, core=None, x=None):
        z = self.z if z is None else z
        y = self.y if y is None else y
        core = self.core if core is None else core
        x = self.x if x is None else x
        return ((z * NY + y) * 2 + core, x)


def remote(src, dst, send, recv, device):
    return pltpu.make_async_remote_copy(
        src_ref=src, dst_ref=dst, send_sem=send, recv_sem=recv, device_id=device, device_id_type=MESH
    )


def hops(d):
    return min(d % NZ, -d % NZ)


def shift(slot):
    return (slot + 6) % SLICES


class Scan:
    def __init__(self, me, state, bufs, reverse):
        (self.other, self.chip, self.plane, self.ahead, self.total, self.planes, self.sums, self.base,
         self.out, self.mine, self.fore, self.result, self.core_sems, self.y_sems, self.z_sems, self.zb_sems,
         self.yb_sems, self.share_sems) = bufs
        self.me, self.state, self.reverse = me, state, reverse
        self.sends = []

    def order(self, count):
        return reversed(range(count)) if self.reverse else range(count)

    def go(self, copy):
        copy.start()
        self.sends.append(copy)
        return copy

    def slice_at(self, slot):
        return lax.rem(self.me.z + shift(slot), SLICES)

    def slot_of(self, j):
        return lax.rem(2 * SLICES + j - 6 - lax.rem(self.me.z, SLICES), SLICES)

    def head_copy(self, d):
        me = self.me
        s = lax.rem(me.y + d, NY)
        return remote(
            self.state.at[HALF * (1 - me.core) + s], self.other.at[s], self.core_sems.at[0, d],
            self.core_sems.at[1, d], me.at(core=1 - me.core)
        )

    def send_head(self, d):
        self.go(self.head_copy(d))

    def y_copy(self, chunk, d):
        me = self.me
        s = lax.rem(me.y + d, NY)
        part = pl.ds(chunk * PART, PART)
        return remote(
            self.chip.at[s, part], self.plane.at[me.y, part], self.y_sems.at[0, chunk, d],
            self.y_sems.at[1, chunk, d], me.at(y=s)
        )

    def y_send(self):
        me = self.me
        for chunk in range(CHUNKS):
            for d in (2, 1, 3, 0):
                s = lax.rem(me.y + d, NY)
                if chunk == 0:
                    self.head_copy(d).wait_recv()
                for slot in range(chunk * PART, chunk * PART + PART):
                    j = self.slice_at(slot)
                    whole = self.state[HALF * me.core + s, j] + self.other[s, j]
                    if d:
                        self.chip[s, slot] = whole
                    else:
                        self.plane[me.y, slot] = whole
                if d:
                    self.go(self.y_copy(chunk, d))

    def z_copy(self, slot, d):
        me = self.me
        d = d % NZ
        z = lax.rem(me.z + d, NZ)
        return remote(
            self.total.at[slot], self.planes.at[me.z], self.z_sems.at[0, d], self.z_sems.at[1, d], me.at(z=z)
        )

    def z_send(self):
        me = self.me
        for chunk in range(CHUNKS):
            for d in (1, 3, 2):
                self.y_copy(chunk, d).wait_recv()
            slots = range(chunk * PART, chunk * PART + PART)
            for slot in slots:
                run = jnp.zeros((DEPTH, HEAD), F32)
                for y in self.order(NY):
                    self.ahead[y, slot] = run
                    run = run + self.plane[y, slot]
                self.total[slot] = run
            targets = [(slot, shift(slot) + far) for slot in slots for far in (0, SLICES)]
            for slot, d in sorted(targets, key=lambda t: -hops(t[1])):
                if d:
                    self.go(self.z_copy(slot, d))
                else:
                    self.planes[me.z] = self.total[slot]

    def zb_copy(self, e):
        me = self.me
        z = lax.rem(me.z + e + NZ, NZ)
        return remote(
            self.sums.at[z], self.base.at[BACK_SLOT[e]], self.zb_sems.at[0, BACK_SLOT[e]],
            self.zb_sems.at[1, BACK_SLOT[e]], me.at(z=z)
        )

    def z_back(self):
        me = self.me
        for d in sorted(range(1, NZ), key=hops):
            self.z_copy(0, d).wait_recv()
        run = jnp.zeros((DEPTH, HEAD), F32)
        for z in self.order(NZ):
            self.sums[z] = run
            run = run + self.planes[z]
        for e in sorted(BACK_SLOT, key=lambda e: -abs(e)):
            if e:
                self.go(self.zb_copy(e))
        self.base[BACK_SLOT[0]] = self.sums[me.z]

    def yb_copy(self, chunk, d):
        me = self.me
        y = lax.rem(me.y + d, NY)
        part = pl.ds(chunk * PART, PART)
        return remote(
            self.out.at[y, part], self.mine.at[me.y, part], self.yb_sems.at[0, chunk, d],
            self.yb_sems.at[1, chunk, d], me.at(y=y)
        )

    def share_copy(self, chunk, d):
        me = self.me
        s = lax.rem(me.y - d + NY, NY)
        part = pl.ds(chunk * PART, PART)
        return remote(
            self.fore.at[s, part], self.result.at[HALF * me.core + s, part], self.share_sems.at[0, chunk, d],
            self.share_sems.at[1, chunk, d], me.at(core=1 - me.core)
        )

    def y_back(self):
        me = self.me
        leads = me.core == (1 if self.reverse else 0)
        for chunk in range(CHUNKS):
            slots = range(chunk * PART, chunk * PART + PART)
            for e, slot in sorted(BACK_SLOT.items(), key=lambda t: abs(t[0])):
                if e and slot in slots:
                    self.zb_copy(e).wait_recv()
            for d in (2, 1, 3, 0):
                y = lax.rem(me.y + d, NY)
                for slot in slots:
                    value = self.ahead[y, slot] + self.base[slot]
                    if d:
                        self.out[y, slot] = value
                    else:
                        self.mine[y, slot] = value
                if d:
                    self.go(self.yb_copy(chunk, d))
        for chunk in range(CHUNKS):
            slots = range(chunk * PART, chunk * PART + PART)
            for d in SHARE_ORDER:
                if d:
                    self.yb_copy(chunk, d).wait_recv()
                s = lax.rem(me.y - d + NY, NY)
                head = HALF * me.core + s
                for slot in slots:
                    j = self.slice_at(slot)
                    got = self.mine[s, slot]
                    self.fore[s, slot] = got + jnp.where(leads, self.state[head, j], 0.0)
                    self.result[head, slot] = got + jnp.where(leads, 0.0, self.other[s, j])
                self.go(self.share_copy(chunk, d))

    def result_head(self, i):
        me = self.me
        d = SHARE_ORDER[i % HALF]
        s = lax.rem(me.y - d + NY, NY)
        if i < HALF:
            return HALF * me.core + s
        for chunk in range(CHUNKS):
            self.share_copy(chunk, d).wait_recv()
        return HALF * (1 - me.core) + s

    def result_state(self, head):
        return jnp.concatenate([self.result[head, self.slot_of(j)] for j in range(SLICES)], 0)

    def finish(self):
        for copy in self.sends:
            copy.wait_send()


def columns(head):
    if isinstance(head, int):
        return pl.ds(head * HEAD, HEAD)
    return pl.ds(pl.multiple_of(head * HEAD, HEAD), HEAD)


def kernel(
    q_hbm, k_hbm, v_hbm, gain_hbm, g_hbm, dq_hbm, dk_hbm, dv_hbm,
    q_raw, k_raw, v_b, g_raw, gain_ref, q_t, q_b, k_b, q_inv, k_inv, att, wei, d_b, scores_b, dk_part, dv_part,
    prior_s, own_s, sums_s, dq_o, dk_o, dv_o, load_sems, store_sems, x_sems, relay, *scan_bufs,
):
    me = Place()
    pairs = []
    for core in (1 - me.core, me.core):
        cols = pl.ds(pl.multiple_of(core * HALF * HEAD, HEAD), HALF * HEAD)
        pairs += [(k_hbm.at[:, cols], k_raw.at[:, cols]), (v_hbm.at[:, cols], v_b.at[:, cols])]
    pairs += [(q_hbm, q_raw), (g_hbm, g_raw), (gain_hbm, gain_ref)]
    loads = [pltpu.make_async_copy(src, dst, load_sems.at[i]) for i, (src, dst) in enumerate(pairs)]
    for copy in loads:
        copy.start()
    barrier = pltpu.get_barrier_semaphore()
    peers = [me.at(core=1 - me.core)]
    peers += [me.at(z=lax.rem(me.z + d, NZ)) for d in FAR_FIRST if hops(d) <= REACH]
    peers += [me.at(y=lax.rem(me.y + d, NY)) for d in (2, 1, 3)]
    peers += [me.at(x=lax.rem(me.x + d, NX)) for d in (2, 1, 3)]
    for peer in peers:
        pl.semaphore_signal(barrier, inc=1, device_id=peer, device_id_type=MESH)

    count = len(scan_bufs) // 2
    fore = Scan(me, own_s.at[0], scan_bufs[:count], False)
    back = Scan(me, own_s.at[1], scan_bufs[count:], True)

    def send_order(i):
        s = lax.rem(me.y + SEND_ORDER[i % HALF], NY)
        return s + HALF * ((1 - me.core) if i < HALF else me.core)

    for i in range(HEADS):
        if i % HALF == 0:
            loads[i // HALF * 2].wait()
            loads[i // HALF * 2 + 1].wait()
        head = send_order(i)
        cols = columns(head)
        wide = k_raw[:, cols].astype(F32)
        inv = lax.rsqrt(jnp.sum(wide * wide, -1, keepdims=True) + 1e-06)
        k_inv[head] = jnp.broadcast_to(inv, (BLOCK, HEAD))
        unit = (wide * inv).astype(BF16)
        k_b[:, cols] = unit
        own_s[0, head] = dot(unit, v_b[:, cols], TN).reshape(SLICES, DEPTH, HEAD)
        if i == HALF - 1:
            pl.semaphore_wait(barrier, len(peers))
            for side, d in enumerate((REACH, NZ - REACH)):
                pl.semaphore_signal(
                    relay.at[side], inc=1, device_id=me.at(z=lax.rem(me.z + d, NZ)), device_id_type=MESH
                )
            for d in SEND_ORDER:
                fore.send_head(d)
    fore.y_send()
    for side in range(2):
        pl.semaphore_wait(relay.at[side], 1)
    fore.z_send()

    for copy in loads[4:]:
        copy.wait()
    lower = lax.broadcasted_iota(jnp.int32, (BLOCK, BLOCK), 0) >= lax.broadcasted_iota(jnp.int32, (BLOCK, BLOCK), 1)
    for head in range(HEADS):
        cols = columns(head)
        wide = q_raw[:, cols].astype(F32)
        inv = lax.rsqrt(jnp.sum(wide * wide, -1, keepdims=True) + 1e-06)
        q_inv[head] = jnp.broadcast_to(inv, (BLOCK, HEAD))
        unit = (wide * inv).astype(BF16)
        q_b[:, cols] = unit
        q_t[head] = unit.T
        scores = jnp.where(lower, dot(unit, k_b[:, cols], NT), 0.0).astype(BF16)
        scores_b[head] = scores
        att[head] = dot(scores, v_b[:, cols], NN)
        wei[head] = g_raw[:, cols].astype(F32) * gain_ref[:, cols]
    fore.z_back()
    fore.y_back()

    square = jnp.zeros((BLOCK, HEAD), F32)
    cross = jnp.zeros((BLOCK, HEAD), F32)
    for i in range(HEADS):
        head = fore.result_head(i)
        both = split(fore.result_state(head), 0)
        prior_s[head] = both
        out = att[head] + dot(twice(q_b[:, columns(head)]), both, NN)
        att[head] = out
        square = square + out * out
        cross = cross + wei[head] * out
    lane = lax.broadcasted_iota(jnp.int32, (BLOCK, HEAD), 1)
    pair = jnp.where(
        lane == 0, jnp.sum(square, -1, keepdims=True), jnp.sum(cross, -1, keepdims=True)
    )
    sums_s[0] = pair.T[:8]
    x_waits = []
    for d in (2, 1, 3):
        copy = remote(
            sums_s.at[0], sums_s.at[d], x_sems.at[0, d], x_sems.at[1, d], me.at(x=lax.rem(me.x + d, NX))
        )
        copy.start()
        x_waits.append(copy)
    for copy in x_waits:
        copy.wait_recv()
    total = (sums_s[0] + sums_s[1]) + (sums_s[2] + sums_s[3])
    full = NX * HEADS * HEAD
    scale = lax.rsqrt(total[0:1] / full + 1e-05)
    slope = total[1:2] * (scale * scale * scale) / full
    row = lax.broadcasted_iota(jnp.int32, (HEAD, BLOCK), 0)
    factors = jnp.where(row == 0, scale, slope).T
    scale, slope = factors[:, 0:1], factors[:, 1:2]

    for i in range(HEADS):
        head = send_order(i)
        cols = columns(head)
        grad = (wei[head] * scale - att[head] * slope).astype(BF16)
        d_b[:, cols] = grad
        own_s[1, head] = dot(q_t[head], grad, NN).reshape(SLICES, DEPTH, HEAD)
        if i < HALF:
            back.send_head(SEND_ORDER[i])
    back.y_send()
    back.z_send()

    for head in range(HEADS):
        cols = columns(head)
        grad = d_b[:, cols]
        keys = k_b[:, cols]
        d_scores = jnp.where(lower, dot(grad, v_b[:, cols], NT), 0.0).astype(BF16)
        d_q = dot(d_scores, keys, NN)
        both = prior_s[head]
        d_q = d_q + dot(twice(grad), jnp.concatenate([both[:HEAD], both[HEAD:]], 1), NT)
        inv = q_inv[head]
        unit = q_raw[:, cols].astype(F32) * inv
        d_q = (d_q - unit * jnp.sum(unit * d_q, -1, keepdims=True)) * inv
        dq_o[:, cols] = d_q.astype(BF16)
        dk_part[head] = dot(d_scores, q_b[:, cols], TN)
        dv_part[head] = dot(scores_b[head], grad, TN)
    stores = [pltpu.make_async_copy(dq_o, dq_hbm, store_sems.at[0])]
    stores[0].start()
    back.z_back()
    back.y_back()

    for i in range(HEADS):
        head = back.result_head(i)
        cols = columns(head)
        state = back.result_state(head)
        keys = k_b[:, cols]
        d_v = dv_part[head] + dot(twice(keys), split(state, 0), NN)
        dv_o[:, cols] = d_v.astype(BF16)
        d_k = dk_part[head] + dot(twice(v_b[:, cols]), split(state, 1), NT)
        inv = k_inv[head]
        unit = k_raw[:, cols].astype(F32) * inv
        d_k = (d_k - unit * jnp.sum(unit * d_k, -1, keepdims=True)) * inv
        dk_o[:, cols] = d_k.astype(BF16)
    stores.append(pltpu.make_async_copy(dk_o, dk_hbm, store_sems.at[1]))
    stores.append(pltpu.make_async_copy(dv_o, dv_hbm, store_sems.at[2]))
    for copy in stores[1:]:
        copy.start()
    fore.finish()
    back.finish()
    for copy in x_waits:
        copy.wait_send()
    for copy in stores:
        copy.wait()


def scan_scratch():
    heads = pltpu.VMEM((HALF, SLICES, DEPTH, HEAD), F32)
    slices = pltpu.VMEM((SLICES, DEPTH, HEAD), F32)
    along_z = pltpu.VMEM((NZ, DEPTH, HEAD), F32)
    sems = pltpu.SemaphoreType.DMA
    return [
        heads, heads, heads, heads, slices, along_z, along_z, slices, heads, heads, heads,
        pltpu.VMEM((HEADS, SLICES, DEPTH, HEAD), F32),
        sems((2, NY)), sems((2, CHUNKS, NY)), sems((2, NZ)), sems((2, SLICES)), sems((2, CHUNKS, NY)),
        sems((2, CHUNKS, NY)),
    ]


def body(query, key, value, gain, grad_out):
    rows, width = query.shape
    flat = pltpu.VMEM((rows, width), BF16)
    wide = pltpu.VMEM((HEADS, rows, HEAD), F32)
    out = jax.ShapeDtypeStruct((rows, width), BF16)
    hbm = pl.BlockSpec(memory_space=pl.ANY)
    grads = pl.pallas_call(
        kernel,
        out_shape=(out, out, out),
        in_specs=[hbm] * 5,
        out_specs=(hbm, hbm, hbm),
        scratch_shapes=[
            flat, flat, flat, flat, pltpu.VMEM((1, width), F32), pltpu.VMEM((HEADS, HEAD, rows), BF16), flat, flat, wide, wide, wide, wide, flat,
            pltpu.VMEM((HEADS, rows, rows), BF16), wide, wide,
            pltpu.VMEM((HEADS, 2 * HEAD, HEAD), BF16),
            pltpu.VMEM((2, HEADS, SLICES, DEPTH, HEAD), F32),
            pltpu.VMEM((NX, 8, rows), F32),
            flat, flat, flat,
            pltpu.SemaphoreType.DMA((7,)), pltpu.SemaphoreType.DMA((3,)), pltpu.SemaphoreType.DMA((2, NX)),
            pltpu.SemaphoreType.REGULAR((2,)),
        ] + scan_scratch() + scan_scratch(),
        compiler_params=pltpu.CompilerParams(
            collective_id=0, has_side_effects=True, vmem_limit_bytes=52 << 20
        ),
        name="linear_attention_backward",
    )(query, key, value, gain.reshape(1, width), grad_out)
    return grads


def solution(mesh):
    placed = (P("ctx", "tp"), P("ctx", "tp"), P("ctx", "tp"), P("tp"), P("ctx", "tp"))
    return jax.shard_map(
        body,
        mesh=mesh,
        in_specs=placed,
        out_specs=(P("ctx", "tp"), P("ctx", "tp"), P("ctx", "tp")),
        check_vma=False,
    )
```

```python
import jax
import jax.numpy as jnp
from jax import lax
from jax.experimental import pallas as pl
from jax.experimental.pallas import tpu as pltpu
from jax.sharding import PartitionSpec as P

HEAD = 128
BLOCK = 256
HEADS = 8
HALF = 4
NY = 4
NZ = 16
NX = 4
SLICES = 8
REACH = (2, 4)
DEPTH = HEAD // SLICES
CHUNKS = 2
PART = SLICES // CHUNKS
F32 = jnp.float32
BF16 = jnp.bfloat16
MESH = pl.DeviceIdType.MESH
FAR_FIRST = sorted(range(1, NZ), key=lambda d: -min(d, NZ - d))
BACK_SLOT = {e: (2 - e) % SLICES for e in range(-4, 4)}
SHARE_ORDER = (0, 1, 3, 2)
SEND_ORDER = (2, 1, 3, 0)

NN = (((1,), (0,)), ((), ()))
NT = (((1,), (1,)), ((), ()))
TN = (((0,), (0,)), ((), ()))


def dot(a, b, dims):
    return lax.dot_general(a, b, dims, preferred_element_type=F32)


def split(wide, axis):
    high = wide.astype(BF16)
    low = (wide - high.astype(F32)).astype(BF16)
    return jnp.concatenate([high, low], axis)


def twice(narrow):
    return jnp.concatenate([narrow, narrow], 1)


class Place:
    def __init__(self):
        ctx = lax.axis_index("ctx")
        self.x = lax.axis_index("tp")
        self.z = lax.div(ctx, 2 * NY)
        self.y = lax.rem(lax.div(ctx, 2), NY)
        self.core = lax.rem(ctx, 2)

    def at(self, z=None, y=None, core=None, x=None):
        z = self.z if z is None else z
        y = self.y if y is None else y
        core = self.core if core is None else core
        x = self.x if x is None else x
        return ((z * NY + y) * 2 + core, x)


def remote(src, dst, send, recv, device):
    return pltpu.make_async_remote_copy(
        src_ref=src, dst_ref=dst, send_sem=send, recv_sem=recv, device_id=device, device_id_type=MESH
    )


def hops(d):
    return min(d % NZ, -d % NZ)


def shift(slot):
    return (slot + 6) % SLICES


class Scan:
    def __init__(self, me, state, bufs, reverse):
        (self.other, self.chip, self.plane, self.ahead, self.total, self.planes, self.sums, self.base,
         self.out, self.mine, self.fore, self.result, self.core_sems, self.y_sems, self.z_sems, self.zb_sems,
         self.yb_sems, self.share_sems) = bufs
        self.me, self.state, self.reverse = me, state, reverse
        self.sends = []

    def order(self, count):
        return reversed(range(count)) if self.reverse else range(count)

    def go(self, copy):
        copy.start()
        self.sends.append(copy)
        return copy

    def slice_at(self, slot):
        return lax.rem(self.me.z + shift(slot), SLICES)

    def slot_of(self, j):
        return lax.rem(2 * SLICES + j - 6 - lax.rem(self.me.z, SLICES), SLICES)

    def head_copy(self, d):
        me = self.me
        s = lax.rem(me.y + d, NY)
        return remote(
            self.state.at[HALF * (1 - me.core) + s], self.other.at[s], self.core_sems.at[0, d],
            self.core_sems.at[1, d], me.at(core=1 - me.core)
        )

    def send_head(self, d):
        self.go(self.head_copy(d))

    def y_copy(self, chunk, d):
        me = self.me
        s = lax.rem(me.y + d, NY)
        part = pl.ds(chunk * PART, PART)
        return remote(
            self.chip.at[s, part], self.plane.at[me.y, part], self.y_sems.at[0, chunk, d],
            self.y_sems.at[1, chunk, d], me.at(y=s)
        )

    def y_send(self):
        me = self.me
        for chunk in range(CHUNKS):
            for d in (2, 1, 3, 0):
                s = lax.rem(me.y + d, NY)
                if chunk == 0:
                    self.head_copy(d).wait_recv()
                for slot in range(chunk * PART, chunk * PART + PART):
                    j = self.slice_at(slot)
                    whole = self.state[HALF * me.core + s, j] + self.other[s, j]
                    if d:
                        self.chip[s, slot] = whole
                    else:
                        self.plane[me.y, slot] = whole
                if d:
                    self.go(self.y_copy(chunk, d))

    def z_copy(self, slot, d):
        me = self.me
        d = d % NZ
        z = lax.rem(me.z + d, NZ)
        return remote(
            self.total.at[slot], self.planes.at[me.z], self.z_sems.at[0, d], self.z_sems.at[1, d], me.at(z=z)
        )

    def z_send(self):
        me = self.me
        for chunk in range(CHUNKS):
            for d in (1, 3, 2):
                self.y_copy(chunk, d).wait_recv()
            slots = range(chunk * PART, chunk * PART + PART)
            for slot in slots:
                run = jnp.zeros((DEPTH, HEAD), F32)
                for y in self.order(NY):
                    self.ahead[y, slot] = run
                    run = run + self.plane[y, slot]
                self.total[slot] = run
            targets = [(slot, shift(slot) + far) for slot in slots for far in (0, SLICES)]
            for slot, d in sorted(targets, key=lambda t: -hops(t[1])):
                if d:
                    self.go(self.z_copy(slot, d))
                else:
                    self.planes[me.z] = self.total[slot]

    def zb_copy(self, e):
        me = self.me
        z = lax.rem(me.z + e + NZ, NZ)
        return remote(
            self.sums.at[z], self.base.at[BACK_SLOT[e]], self.zb_sems.at[0, BACK_SLOT[e]],
            self.zb_sems.at[1, BACK_SLOT[e]], me.at(z=z)
        )

    def z_back(self):
        me = self.me
        for d in sorted(range(1, NZ), key=hops):
            self.z_copy(0, d).wait_recv()
        run = jnp.zeros((DEPTH, HEAD), F32)
        for z in self.order(NZ):
            self.sums[z] = run
            run = run + self.planes[z]
        for e in sorted(BACK_SLOT, key=lambda e: -abs(e)):
            if e:
                self.go(self.zb_copy(e))
        self.base[BACK_SLOT[0]] = self.sums[me.z]

    def yb_copy(self, chunk, d):
        me = self.me
        y = lax.rem(me.y + d, NY)
        part = pl.ds(chunk * PART, PART)
        return remote(
            self.out.at[y, part], self.mine.at[me.y, part], self.yb_sems.at[0, chunk, d],
            self.yb_sems.at[1, chunk, d], me.at(y=y)
        )

    def share_copy(self, chunk, d):
        me = self.me
        s = lax.rem(me.y - d + NY, NY)
        part = pl.ds(chunk * PART, PART)
        return remote(
            self.fore.at[s, part], self.result.at[HALF * me.core + s, part], self.share_sems.at[0, chunk, d],
            self.share_sems.at[1, chunk, d], me.at(core=1 - me.core)
        )

    def y_back(self):
        me = self.me
        leads = me.core == (1 if self.reverse else 0)
        for chunk in range(CHUNKS):
            slots = range(chunk * PART, chunk * PART + PART)
            for e, slot in sorted(BACK_SLOT.items(), key=lambda t: abs(t[0])):
                if e and slot in slots:
                    self.zb_copy(e).wait_recv()
            for d in (2, 1, 3, 0):
                y = lax.rem(me.y + d, NY)
                for slot in slots:
                    value = self.ahead[y, slot] + self.base[slot]
                    if d:
                        self.out[y, slot] = value
                    else:
                        self.mine[y, slot] = value
                if d:
                    self.go(self.yb_copy(chunk, d))
        self.drain()
        for chunk in range(CHUNKS):
            slots = range(chunk * PART, chunk * PART + PART)
            for d in SHARE_ORDER:
                if d:
                    self.yb_copy(chunk, d).wait_recv()
                s = lax.rem(me.y - d + NY, NY)
                head = HALF * me.core + s
                for slot in slots:
                    j = self.slice_at(slot)
                    got = self.mine[s, slot]
                    self.fore[s, slot] = got + jnp.where(leads, self.state[head, j], 0.0)
                    self.result[head, slot] = got + jnp.where(leads, 0.0, self.other[s, j])
                self.go(self.share_copy(chunk, d))

    def result_head(self, i):
        me = self.me
        d = SHARE_ORDER[i % HALF]
        s = lax.rem(me.y - d + NY, NY)
        if i < HALF:
            return HALF * me.core + s
        for chunk in range(CHUNKS):
            self.share_copy(chunk, d).wait_recv()
        return HALF * (1 - me.core) + s

    def result_state(self, head):
        return jnp.concatenate([self.result[head, self.slot_of(j)] for j in range(SLICES)], 0)

    def drain(self):
        for copy in self.sends:
            copy.wait_send()
        self.sends = []


def vouch(me, relay, step):
    for side, d in enumerate((REACH[step], NZ - REACH[step])):
        pl.semaphore_signal(
            relay.at[step, side], inc=1, device_id=me.at(z=lax.rem(me.z + d, NZ)), device_id_type=MESH
        )


def heard(relay, step):
    for side in range(2):
        pl.semaphore_wait(relay.at[step, side], 1)


def columns(head):
    if isinstance(head, int):
        return pl.ds(head * HEAD, HEAD)
    return pl.ds(pl.multiple_of(head * HEAD, HEAD), HEAD)


def kernel(
    q_hbm, k_hbm, v_hbm, gain_hbm, g_hbm, dq_o, dk_o, dv_o,
    q_raw, k_raw, v_b, g_raw, gain_ref, q_t, q_b, k_b, q_inv, k_inv, att, wei, d_b, scores_b, dk_part, dv_part,
    prior_s, own_s, sums_s, load_sems, x_sems, relay, *scan_bufs,
):
    me = Place()
    pairs = []
    for core in (1 - me.core, me.core):
        cols = pl.ds(pl.multiple_of(core * HALF * HEAD, HEAD), HALF * HEAD)
        pairs += [(k_hbm.at[:, cols], k_raw.at[:, cols]), (v_hbm.at[:, cols], v_b.at[:, cols])]
    pairs += [(q_hbm, q_raw), (g_hbm, g_raw), (gain_hbm, gain_ref)]
    loads = [pltpu.make_async_copy(src, dst, load_sems.at[i]) for i, (src, dst) in enumerate(pairs)]
    for copy in loads:
        copy.start()
    barrier = pltpu.get_barrier_semaphore()
    peers = [me.at(core=1 - me.core)]
    peers += [me.at(z=lax.rem(me.z + d, NZ)) for d in FAR_FIRST if hops(d) <= REACH[0]]
    peers += [me.at(y=lax.rem(me.y + d, NY)) for d in (2, 1, 3)]
    peers += [me.at(x=lax.rem(me.x + d, NX)) for d in (2, 1, 3)]
    for peer in peers:
        pl.semaphore_signal(barrier, inc=1, device_id=peer, device_id_type=MESH)

    count = len(scan_bufs) // 2
    fore = Scan(me, own_s.at[0], scan_bufs[:count], False)
    back = Scan(me, own_s.at[1], scan_bufs[count:], True)

    def send_order(i):
        s = lax.rem(me.y + SEND_ORDER[i % HALF], NY)
        return s + HALF * ((1 - me.core) if i < HALF else me.core)

    for i in range(HEADS):
        if i % HALF == 0:
            loads[i // HALF * 2].wait()
            loads[i // HALF * 2 + 1].wait()
        head = send_order(i)
        cols = columns(head)
        wide = k_raw[:, cols].astype(F32)
        inv = lax.rsqrt(jnp.sum(wide * wide, -1, keepdims=True) + 1e-06)
        k_inv[head] = jnp.broadcast_to(inv, (BLOCK, HEAD))
        unit = (wide * inv).astype(BF16)
        k_b[:, cols] = unit
        own_s[0, head] = dot(unit, v_b[:, cols], TN).reshape(SLICES, DEPTH, HEAD)
        if i == HALF - 1:
            pl.semaphore_wait(barrier, len(peers))
            vouch(me, relay, 0)
            for d in SEND_ORDER:
                fore.send_head(d)
    heard(relay, 0)
    vouch(me, relay, 1)
    fore.y_send()
    heard(relay, 1)
    fore.z_send()

    for copy in loads[4:]:
        copy.wait()
    lower = lax.broadcasted_iota(jnp.int32, (BLOCK, BLOCK), 0) >= lax.broadcasted_iota(jnp.int32, (BLOCK, BLOCK), 1)
    for head in range(HEADS):
        cols = columns(head)
        wide = q_raw[:, cols].astype(F32)
        inv = lax.rsqrt(jnp.sum(wide * wide, -1, keepdims=True) + 1e-06)
        q_inv[head] = jnp.broadcast_to(inv, (BLOCK, HEAD))
        unit = (wide * inv).astype(BF16)
        q_b[:, cols] = unit
        q_t[head] = unit.T
        scores = jnp.where(lower, dot(unit, k_b[:, cols], NT), 0.0).astype(BF16)
        scores_b[head] = scores
        att[head] = dot(scores, v_b[:, cols], NN)
        wei[head] = g_raw[:, cols].astype(F32) * gain_ref[:, cols]
    fore.z_back()
    fore.y_back()

    square = jnp.zeros((BLOCK, HEAD), F32)
    cross = jnp.zeros((BLOCK, HEAD), F32)
    for i in range(HEADS):
        head = fore.result_head(i)
        both = split(fore.result_state(head), 0)
        prior_s[head] = both
        out = att[head] + dot(twice(q_b[:, columns(head)]), both, NN)
        att[head] = out
        square = square + out * out
        cross = cross + wei[head] * out
    lane = lax.broadcasted_iota(jnp.int32, (BLOCK, HEAD), 1)
    pair = jnp.where(
        lane == 0, jnp.sum(square, -1, keepdims=True), jnp.sum(cross, -1, keepdims=True)
    )
    sums_s[0] = pair.T[:8]
    x_waits = []
    for d in (2, 1, 3):
        copy = remote(
            sums_s.at[0], sums_s.at[d], x_sems.at[0, d], x_sems.at[1, d], me.at(x=lax.rem(me.x + d, NX))
        )
        copy.start()
        x_waits.append(copy)
    for copy in x_waits:
        copy.wait_recv()
    total = (sums_s[0] + sums_s[1]) + (sums_s[2] + sums_s[3])
    full = NX * HEADS * HEAD
    scale = lax.rsqrt(total[0:1] / full + 1e-05)
    slope = total[1:2] * (scale * scale * scale) / full
    row = lax.broadcasted_iota(jnp.int32, (HEAD, BLOCK), 0)
    factors = jnp.where(row == 0, scale, slope).T
    scale, slope = factors[:, 0:1], factors[:, 1:2]

    for i in range(HEADS):
        head = send_order(i)
        cols = columns(head)
        grad = (wei[head] * scale - att[head] * slope).astype(BF16)
        d_b[:, cols] = grad
        own_s[1, head] = dot(q_t[head], grad, NN).reshape(SLICES, DEPTH, HEAD)
        if i < HALF:
            back.send_head(SEND_ORDER[i])
    back.y_send()
    back.z_send()

    for head in range(HEADS):
        cols = columns(head)
        grad = d_b[:, cols]
        keys = k_b[:, cols]
        d_scores = jnp.where(lower, dot(grad, v_b[:, cols], NT), 0.0).astype(BF16)
        d_q = dot(d_scores, keys, NN)
        both = prior_s[head]
        d_q = d_q + dot(twice(grad), jnp.concatenate([both[:HEAD], both[HEAD:]], 1), NT)
        inv = q_inv[head]
        unit = q_raw[:, cols].astype(F32) * inv
        d_q = (d_q - unit * jnp.sum(unit * d_q, -1, keepdims=True)) * inv
        dq_o[:, cols] = d_q.astype(BF16)
        dk_part[head] = dot(d_scores, q_b[:, cols], TN)
        dv_part[head] = dot(scores_b[head], grad, TN)
    fore.drain()
    for copy in x_waits:
        copy.wait_send()
    back.drain()
    back.z_back()
    back.y_back()

    for i in range(HEADS):
        head = back.result_head(i)
        cols = columns(head)
        state = back.result_state(head)
        keys = k_b[:, cols]
        d_v = dv_part[head] + dot(twice(keys), split(state, 0), NN)
        dv_o[:, cols] = d_v.astype(BF16)
        d_k = dk_part[head] + dot(twice(v_b[:, cols]), split(state, 1), NT)
        inv = k_inv[head]
        unit = k_raw[:, cols].astype(F32) * inv
        d_k = (d_k - unit * jnp.sum(unit * d_k, -1, keepdims=True)) * inv
        dk_o[:, cols] = d_k.astype(BF16)
    back.drain()


def scan_scratch():
    heads = pltpu.VMEM((HALF, SLICES, DEPTH, HEAD), F32)
    slices = pltpu.VMEM((SLICES, DEPTH, HEAD), F32)
    along_z = pltpu.VMEM((NZ, DEPTH, HEAD), F32)
    sems = pltpu.SemaphoreType.DMA
    return [
        heads, heads, heads, heads, slices, along_z, along_z, slices, heads, heads, heads,
        pltpu.VMEM((HEADS, SLICES, DEPTH, HEAD), F32),
        sems((2, NY)), sems((2, CHUNKS, NY)), sems((2, NZ)), sems((2, SLICES)), sems((2, CHUNKS, NY)),
        sems((2, CHUNKS, NY)),
    ]


def body(query, key, value, gain, grad_out):
    rows, width = query.shape
    flat = pltpu.VMEM((rows, width), BF16)
    wide = pltpu.VMEM((HEADS, rows, HEAD), F32)
    out = jax.ShapeDtypeStruct((rows, width), BF16)
    hbm = pl.BlockSpec(memory_space=pl.ANY)
    grads = pl.pallas_call(
        kernel,
        out_shape=(out, out, out),
        in_specs=[hbm] * 5,
        out_specs=(pl.BlockSpec(memory_space=pltpu.VMEM),) * 3,
        scratch_shapes=[
            flat, flat, flat, flat, pltpu.VMEM((1, width), F32), pltpu.VMEM((HEADS, HEAD, rows), BF16), flat, flat, wide, wide, wide, wide, flat,
            pltpu.VMEM((HEADS, rows, rows), BF16), wide, wide,
            pltpu.VMEM((HEADS, 2 * HEAD, HEAD), BF16),
            pltpu.VMEM((2, HEADS, SLICES, DEPTH, HEAD), F32),
            pltpu.VMEM((NX, 8, rows), F32),
            pltpu.SemaphoreType.DMA((7,)), pltpu.SemaphoreType.DMA((2, NX)),
            pltpu.SemaphoreType.REGULAR((2, 2)),
        ] + scan_scratch() + scan_scratch(),
        compiler_params=pltpu.CompilerParams(
            collective_id=0, has_side_effects=True, vmem_limit_bytes=52 << 20
        ),
        name="linear_attention_backward",
    )(query, key, value, gain.reshape(1, width), grad_out)
    return grads


def solution(mesh):
    placed = (P("ctx", "tp"), P("ctx", "tp"), P("ctx", "tp"), P("tp"), P("ctx", "tp"))
    return jax.shard_map(
        body,
        mesh=mesh,
        in_specs=placed,
        out_specs=(P("ctx", "tp"), P("ctx", "tp"), P("ctx", "tp")),
        check_vma=False,
    )
```

```python
import jax
import jax.numpy as jnp
from jax import lax
from jax.experimental import pallas as pl
from jax.experimental.pallas import tpu as pltpu
from jax.sharding import PartitionSpec as P

HEAD = 128
BLOCK = 256
HEADS = 8
HALF = 4
NY = 4
NZ = 16
NX = 4
SLICES = 8
REACH = (2, 4)
LEAST = 4
DEPTH = HEAD // SLICES
CHUNKS = 2
PART = SLICES // CHUNKS
F32 = jnp.float32
BF16 = jnp.bfloat16
MESH = pl.DeviceIdType.MESH
FAR_FIRST = sorted(range(1, NZ), key=lambda d: -min(d, NZ - d))
BACK_SLOT = {e: (2 - e) % SLICES for e in range(-4, 4)}
SHARE_ORDER = (0, 1, 3, 2)
SEND_ORDER = (2, 1, 3, 0)

NN = (((1,), (0,)), ((), ()))
NT = (((1,), (1,)), ((), ()))
TN = (((0,), (0,)), ((), ()))


def dot(a, b, dims):
    return lax.dot_general(a, b, dims, preferred_element_type=F32)


def split(wide, axis):
    high = wide.astype(BF16)
    low = (wide - high.astype(F32)).astype(BF16)
    return jnp.concatenate([high, low], axis)


def twice(narrow):
    return jnp.concatenate([narrow, narrow], 1)


class Place:
    def __init__(self):
        ctx = lax.axis_index("ctx")
        self.x = lax.axis_index("tp")
        self.z = lax.div(ctx, 2 * NY)
        self.y = lax.rem(lax.div(ctx, 2), NY)
        self.core = lax.rem(ctx, 2)

    def at(self, z=None, y=None, core=None, x=None):
        z = self.z if z is None else z
        y = self.y if y is None else y
        core = self.core if core is None else core
        x = self.x if x is None else x
        return ((z * NY + y) * 2 + core, x)


def remote(src, dst, send, recv, device):
    return pltpu.make_async_remote_copy(
        src_ref=src, dst_ref=dst, send_sem=send, recv_sem=recv, device_id=device, device_id_type=MESH
    )


def hops(d):
    return min(d % NZ, -d % NZ)


def shift(slot):
    return (slot + 6) % SLICES


class Scan:
    def __init__(self, me, state, bufs, reverse):
        (self.other, self.chip, self.plane, self.ahead, self.total, self.planes, self.sums, self.base,
         self.out, self.mine, self.fore, self.result, self.core_sems, self.y_sems, self.z_sems, self.zb_sems,
         self.yb_sems, self.share_sems) = bufs
        self.me, self.state, self.reverse = me, state, reverse
        self.sends = []

    def order(self, count):
        return reversed(range(count)) if self.reverse else range(count)

    def go(self, copy):
        copy.start()
        self.sends.append(copy)
        return copy

    def slice_at(self, slot):
        return lax.rem(self.me.z + shift(slot), SLICES)

    def slot_of(self, j):
        return lax.rem(2 * SLICES + j - 6 - lax.rem(self.me.z, SLICES), SLICES)

    def head_copy(self, d):
        me = self.me
        s = lax.rem(me.y + d, NY)
        return remote(
            self.state.at[HALF * (1 - me.core) + s], self.other.at[s], self.core_sems.at[0, d],
            self.core_sems.at[1, d], me.at(core=1 - me.core)
        )

    def send_head(self, d):
        self.go(self.head_copy(d))

    def y_copy(self, chunk, d):
        me = self.me
        s = lax.rem(me.y + d, NY)
        part = pl.ds(chunk * PART, PART)
        return remote(
            self.chip.at[s, part], self.plane.at[me.y, part], self.y_sems.at[0, chunk, d],
            self.y_sems.at[1, chunk, d], me.at(y=s)
        )

    def y_send(self):
        me = self.me
        for chunk in range(CHUNKS):
            for d in (2, 1, 3, 0):
                s = lax.rem(me.y + d, NY)
                if chunk == 0:
                    self.head_copy(d).wait_recv()
                for slot in range(chunk * PART, chunk * PART + PART):
                    j = self.slice_at(slot)
                    whole = self.state[HALF * me.core + s, j] + self.other[s, j]
                    if d:
                        self.chip[s, slot] = whole
                    else:
                        self.plane[me.y, slot] = whole
                if d:
                    self.go(self.y_copy(chunk, d))

    def z_copy(self, slot, d):
        me = self.me
        d = d % NZ
        z = lax.rem(me.z + d, NZ)
        return remote(
            self.total.at[slot], self.planes.at[me.z], self.z_sems.at[0, d], self.z_sems.at[1, d], me.at(z=z)
        )

    def z_send(self):
        me = self.me
        targets = []
        for chunk in range(CHUNKS):
            for d in (1, 3, 2):
                self.y_copy(chunk, d).wait_recv()
            slots = range(chunk * PART, chunk * PART + PART)
            for slot in slots:
                run = jnp.zeros((DEPTH, HEAD), F32)
                for y in self.order(NY):
                    self.ahead[y, slot] = run
                    run = run + self.plane[y, slot]
                self.total[slot] = run
            targets += [(slot, shift(slot) + far) for slot in slots for far in (0, SLICES)]
            ready = [t for t in targets if hops(t[1]) >= LEAST or chunk == CHUNKS - 1]
            targets = [t for t in targets if t not in ready]
            for slot, d in sorted(ready, key=lambda t: -hops(t[1])):
                if d:
                    self.go(self.z_copy(slot, d))
                else:
                    self.planes[me.z] = self.total[slot]

    def zb_copy(self, e):
        me = self.me
        z = lax.rem(me.z + e + NZ, NZ)
        return remote(
            self.sums.at[z], self.base.at[BACK_SLOT[e]], self.zb_sems.at[0, BACK_SLOT[e]],
            self.zb_sems.at[1, BACK_SLOT[e]], me.at(z=z)
        )

    def z_back(self):
        me = self.me
        for d in sorted(range(1, NZ), key=hops):
            self.z_copy(0, d).wait_recv()
        run = jnp.zeros((DEPTH, HEAD), F32)
        for z in self.order(NZ):
            self.sums[z] = run
            run = run + self.planes[z]
        for e in sorted(BACK_SLOT, key=lambda e: -abs(e)):
            if e:
                self.go(self.zb_copy(e))
        self.base[BACK_SLOT[0]] = self.sums[me.z]

    def yb_copy(self, chunk, d):
        me = self.me
        y = lax.rem(me.y + d, NY)
        part = pl.ds(chunk * PART, PART)
        return remote(
            self.out.at[y, part], self.mine.at[me.y, part], self.yb_sems.at[0, chunk, d],
            self.yb_sems.at[1, chunk, d], me.at(y=y)
        )

    def share_copy(self, chunk, d):
        me = self.me
        s = lax.rem(me.y - d + NY, NY)
        part = pl.ds(chunk * PART, PART)
        return remote(
            self.fore.at[s, part], self.result.at[HALF * me.core + s, part], self.share_sems.at[0, chunk, d],
            self.share_sems.at[1, chunk, d], me.at(core=1 - me.core)
        )

    def y_back(self):
        me = self.me
        leads = me.core == (1 if self.reverse else 0)
        for chunk in range(CHUNKS):
            slots = range(chunk * PART, chunk * PART + PART)
            for e, slot in sorted(BACK_SLOT.items(), key=lambda t: abs(t[0])):
                if e and slot in slots:
                    self.zb_copy(e).wait_recv()
            for d in (2, 1, 3, 0):
                y = lax.rem(me.y + d, NY)
                for slot in slots:
                    value = self.ahead[y, slot] + self.base[slot]
                    if d:
                        self.out[y, slot] = value
                    else:
                        self.mine[y, slot] = value
                if d:
                    self.go(self.yb_copy(chunk, d))
        self.drain()
        for chunk in range(CHUNKS):
            slots = range(chunk * PART, chunk * PART + PART)
            for d in SHARE_ORDER:
                if d:
                    self.yb_copy(chunk, d).wait_recv()
                s = lax.rem(me.y - d + NY, NY)
                head = HALF * me.core + s
                for slot in slots:
                    j = self.slice_at(slot)
                    got = self.mine[s, slot]
                    self.fore[s, slot] = got + jnp.where(leads, self.state[head, j], 0.0)
                    self.result[head, slot] = got + jnp.where(leads, 0.0, self.other[s, j])
                self.go(self.share_copy(chunk, d))

    def result_head(self, i):
        me = self.me
        d = SHARE_ORDER[i % HALF]
        s = lax.rem(me.y - d + NY, NY)
        if i < HALF:
            return HALF * me.core + s
        for chunk in range(CHUNKS):
            self.share_copy(chunk, d).wait_recv()
        return HALF * (1 - me.core) + s

    def result_state(self, head):
        return jnp.concatenate([self.result[head, self.slot_of(j)] for j in range(SLICES)], 0)

    def drain(self):
        for copy in self.sends:
            copy.wait_send()
        self.sends = []


def vouch(me, relay, step):
    for side, d in enumerate((REACH[step], NZ - REACH[step])):
        pl.semaphore_signal(
            relay.at[step, side], inc=1, device_id=me.at(z=lax.rem(me.z + d, NZ)), device_id_type=MESH
        )


def heard(relay, step):
    for side in range(2):
        pl.semaphore_wait(relay.at[step, side], 1)


def columns(head):
    if isinstance(head, int):
        return pl.ds(head * HEAD, HEAD)
    return pl.ds(pl.multiple_of(head * HEAD, HEAD), HEAD)


def kernel(
    q_hbm, k_hbm, v_hbm, gain_hbm, g_hbm, dq_o, dk_o, dv_o,
    q_raw, k_raw, v_b, g_raw, gain_ref, q_t, q_b, k_b, q_inv, k_inv, att, wei, d_b, scores_b, dk_part, dv_part,
    prior_s, own_s, sums_s, load_sems, x_sems, relay, *scan_bufs,
):
    me = Place()
    pairs = []
    for core in (1 - me.core, me.core):
        cols = pl.ds(pl.multiple_of(core * HALF * HEAD, HEAD), HALF * HEAD)
        pairs += [(k_hbm.at[:, cols], k_raw.at[:, cols]), (v_hbm.at[:, cols], v_b.at[:, cols])]
    pairs += [(q_hbm, q_raw), (g_hbm, g_raw), (gain_hbm, gain_ref)]
    loads = [pltpu.make_async_copy(src, dst, load_sems.at[i]) for i, (src, dst) in enumerate(pairs)]
    for copy in loads:
        copy.start()
    barrier = pltpu.get_barrier_semaphore()
    peers = [me.at(core=1 - me.core)]
    peers += [me.at(z=lax.rem(me.z + d, NZ)) for d in FAR_FIRST if hops(d) <= REACH[0]]
    peers += [me.at(y=lax.rem(me.y + d, NY)) for d in (2, 1, 3)]
    peers += [me.at(x=lax.rem(me.x + d, NX)) for d in (2, 1, 3)]
    for peer in peers:
        pl.semaphore_signal(barrier, inc=1, device_id=peer, device_id_type=MESH)

    count = len(scan_bufs) // 2
    fore = Scan(me, own_s.at[0], scan_bufs[:count], False)
    back = Scan(me, own_s.at[1], scan_bufs[count:], True)

    def send_order(i):
        s = lax.rem(me.y + SEND_ORDER[i % HALF], NY)
        return s + HALF * ((1 - me.core) if i < HALF else me.core)

    for i in range(HEADS):
        if i % HALF == 0:
            loads[i // HALF * 2].wait()
            loads[i // HALF * 2 + 1].wait()
        head = send_order(i)
        cols = columns(head)
        wide = k_raw[:, cols].astype(F32)
        inv = lax.rsqrt(jnp.sum(wide * wide, -1, keepdims=True) + 1e-06)
        k_inv[head] = jnp.broadcast_to(inv, (BLOCK, HEAD))
        unit = (wide * inv).astype(BF16)
        k_b[:, cols] = unit
        own_s[0, head] = dot(unit, v_b[:, cols], TN).reshape(SLICES, DEPTH, HEAD)
        if i == HALF - 1:
            pl.semaphore_wait(barrier, len(peers))
            vouch(me, relay, 0)
            for d in SEND_ORDER:
                fore.send_head(d)
    heard(relay, 0)
    vouch(me, relay, 1)
    fore.y_send()
    heard(relay, 1)
    fore.z_send()

    for copy in loads[4:]:
        copy.wait()
    lower = lax.broadcasted_iota(jnp.int32, (BLOCK, BLOCK), 0) >= lax.broadcasted_iota(jnp.int32, (BLOCK, BLOCK), 1)
    for head in range(HEADS):
        cols = columns(head)
        wide = q_raw[:, cols].astype(F32)
        inv = lax.rsqrt(jnp.sum(wide * wide, -1, keepdims=True) + 1e-06)
        q_inv[head] = jnp.broadcast_to(inv, (BLOCK, HEAD))
        unit = (wide * inv).astype(BF16)
        q_b[:, cols] = unit
        q_t[head] = unit.T
        scores = jnp.where(lower, dot(unit, k_b[:, cols], NT), 0.0).astype(BF16)
        scores_b[head] = scores
        att[head] = dot(scores, v_b[:, cols], NN)
        wei[head] = g_raw[:, cols].astype(F32) * gain_ref[:, cols]
    fore.z_back()
    fore.y_back()

    square = jnp.zeros((BLOCK, HEAD), F32)
    cross = jnp.zeros((BLOCK, HEAD), F32)
    for i in range(HEADS):
        head = fore.result_head(i)
        both = split(fore.result_state(head), 0)
        prior_s[head] = both
        out = att[head] + dot(twice(q_b[:, columns(head)]), both, NN)
        att[head] = out
        square = square + out * out
        cross = cross + wei[head] * out
    lane = lax.broadcasted_iota(jnp.int32, (BLOCK, HEAD), 1)
    pair = jnp.where(
        lane == 0, jnp.sum(square, -1, keepdims=True), jnp.sum(cross, -1, keepdims=True)
    )
    sums_s[0] = pair.T[:8]
    x_waits = []
    for d in (2, 1, 3):
        copy = remote(
            sums_s.at[0], sums_s.at[d], x_sems.at[0, d], x_sems.at[1, d], me.at(x=lax.rem(me.x + d, NX))
        )
        copy.start()
        x_waits.append(copy)
    for copy in x_waits:
        copy.wait_recv()
    total = (sums_s[0] + sums_s[1]) + (sums_s[2] + sums_s[3])
    full = NX * HEADS * HEAD
    scale = lax.rsqrt(total[0:1] / full + 1e-05)
    slope = total[1:2] * (scale * scale * scale) / full
    row = lax.broadcasted_iota(jnp.int32, (HEAD, BLOCK), 0)
    factors = jnp.where(row == 0, scale, slope).T
    scale, slope = factors[:, 0:1], factors[:, 1:2]

    for i in range(HEADS):
        head = send_order(i)
        cols = columns(head)
        grad = (wei[head] * scale - att[head] * slope).astype(BF16)
        d_b[:, cols] = grad
        own_s[1, head] = dot(q_t[head], grad, NN).reshape(SLICES, DEPTH, HEAD)
        if i < HALF:
            back.send_head(SEND_ORDER[i])
    back.y_send()
    back.z_send()

    for head in range(HEADS):
        cols = columns(head)
        grad = d_b[:, cols]
        keys = k_b[:, cols]
        d_scores = jnp.where(lower, dot(grad, v_b[:, cols], NT), 0.0).astype(BF16)
        d_q = dot(d_scores, keys, NN)
        both = prior_s[head]
        d_q = d_q + dot(twice(grad), jnp.concatenate([both[:HEAD], both[HEAD:]], 1), NT)
        inv = q_inv[head]
        unit = q_raw[:, cols].astype(F32) * inv
        d_q = (d_q - unit * jnp.sum(unit * d_q, -1, keepdims=True)) * inv
        dq_o[:, cols] = d_q.astype(BF16)
        dk_part[head] = dot(d_scores, q_b[:, cols], TN)
        dv_part[head] = dot(scores_b[head], grad, TN)
    fore.drain()
    for copy in x_waits:
        copy.wait_send()
    back.drain()
    back.z_back()
    back.y_back()

    for i in range(HEADS):
        head = back.result_head(i)
        cols = columns(head)
        state = back.result_state(head)
        keys = k_b[:, cols]
        d_v = dv_part[head] + dot(twice(keys), split(state, 0), NN)
        dv_o[:, cols] = d_v.astype(BF16)
        d_k = dk_part[head] + dot(twice(v_b[:, cols]), split(state, 1), NT)
        inv = k_inv[head]
        unit = k_raw[:, cols].astype(F32) * inv
        d_k = (d_k - unit * jnp.sum(unit * d_k, -1, keepdims=True)) * inv
        dk_o[:, cols] = d_k.astype(BF16)
    back.drain()


def scan_scratch():
    heads = pltpu.VMEM((HALF, SLICES, DEPTH, HEAD), F32)
    slices = pltpu.VMEM((SLICES, DEPTH, HEAD), F32)
    along_z = pltpu.VMEM((NZ, DEPTH, HEAD), F32)
    sems = pltpu.SemaphoreType.DMA
    return [
        heads, heads, heads, heads, slices, along_z, along_z, slices, heads, heads, heads,
        pltpu.VMEM((HEADS, SLICES, DEPTH, HEAD), F32),
        sems((2, NY)), sems((2, CHUNKS, NY)), sems((2, NZ)), sems((2, SLICES)), sems((2, CHUNKS, NY)),
        sems((2, CHUNKS, NY)),
    ]


def body(query, key, value, gain, grad_out):
    rows, width = query.shape
    flat = pltpu.VMEM((rows, width), BF16)
    wide = pltpu.VMEM((HEADS, rows, HEAD), F32)
    out = jax.ShapeDtypeStruct((rows, width), BF16)
    hbm = pl.BlockSpec(memory_space=pl.ANY)
    grads = pl.pallas_call(
        kernel,
        out_shape=(out, out, out),
        in_specs=[hbm] * 5,
        out_specs=(pl.BlockSpec(memory_space=pltpu.VMEM),) * 3,
        scratch_shapes=[
            flat, flat, flat, flat, pltpu.VMEM((1, width), F32), pltpu.VMEM((HEADS, HEAD, rows), BF16), flat, flat, wide, wide, wide, wide, flat,
            pltpu.VMEM((HEADS, rows, rows), BF16), wide, wide,
            pltpu.VMEM((HEADS, 2 * HEAD, HEAD), BF16),
            pltpu.VMEM((2, HEADS, SLICES, DEPTH, HEAD), F32),
            pltpu.VMEM((NX, 8, rows), F32),
            pltpu.SemaphoreType.DMA((7,)), pltpu.SemaphoreType.DMA((2, NX)),
            pltpu.SemaphoreType.REGULAR((2, 2)),
        ] + scan_scratch() + scan_scratch(),
        compiler_params=pltpu.CompilerParams(
            collective_id=0, has_side_effects=True, vmem_limit_bytes=52 << 20
        ),
        name="linear_attention_backward",
    )(query, key, value, gain.reshape(1, width), grad_out)
    return grads


def solution(mesh):
    placed = (P("ctx", "tp"), P("ctx", "tp"), P("ctx", "tp"), P("tp"), P("ctx", "tp"))
    return jax.shard_map(
        body,
        mesh=mesh,
        in_specs=placed,
        out_specs=(P("ctx", "tp"), P("ctx", "tp"), P("ctx", "tp")),
        check_vma=False,
    )
```
